256 devices in a mesh: leaf: 64 (over y, x, z_hi), head: 4 (over z_lo, core).
Axes of the slice: x: 4, y: 4, z: 8 (z_hi: 4, z_lo: 2; z = z_hi * 2 + z_lo), core: 2. Of those that a mesh axis runs over, the one named last changes fastest.
Arguments:
- root_query: bfloat16 [1024, 8192], P('leaf', 'head'), may hold values from -6 to 6
- branch_query: bfloat16 [4096, 8192], P('leaf', 'head'), may hold values from -6 to 6
- leaf_query: bfloat16 [8192, 8192], P('leaf', 'head'), may hold values from -8 to 8
- root_key: bfloat16 [1024, 1024], P(('leaf', 'head')), may hold values from -6 to 6
- root_value: bfloat16 [1024, 1024], P(('leaf', 'head')), may hold values from -6 to 6
- branch_key: bfloat16 [4096, 1024], P('leaf', 'head'), may hold values from -6 to 6
- branch_value: bfloat16 [4096, 1024], P('leaf', 'head'), may hold values from -6 to 6
- leaf_key: bfloat16 [8192, 1024], P('leaf', 'head'), may hold values from -8 to 8
- leaf_value: bfloat16 [8192, 1024], P('leaf', 'head'), may hold values from -6 to 6
- root_grad_out: bfloat16 [1024, 8192], P('leaf', 'head'), may hold values from -6 to 6
- branch_grad_out: bfloat16 [4096, 8192], P('leaf', 'head'), may hold values from -6 to 6
- leaf_grad_out: bfloat16 [8192, 8192], P('leaf', 'head'), may hold values from -6 to 6
- branch_lengths: int32 [8], replicated, may hold values from 1 to 512, 2901 in all
- leaf_lengths: int32 [64], P('leaf'), may hold values from 1 to 128, 5504 in all
Outputs:
- root_attended: bfloat16 [1024, 8192], P('leaf', 'head')
- branch_attended: bfloat16 [4096, 8192], P('leaf', 'head')
- leaf_attended: bfloat16 [8192, 8192], P('leaf', 'head')
- root_query_grad: bfloat16 [1024, 8192], P('leaf', 'head')
- branch_query_grad: bfloat16 [4096, 8192], P('leaf', 'head')
- leaf_query_grad: bfloat16 [8192, 8192], P('leaf', 'head')
- root_key_grad: bfloat16 [1024, 1024], P(('leaf', 'head'))
- root_value_grad: bfloat16 [1024, 1024], P(('leaf', 'head'))
- branch_key_grad: bfloat16 [4096, 1024], P('leaf', 'head')
- branch_value_grad: bfloat16 [4096, 1024], P('leaf', 'head')
- leaf_key_grad: bfloat16 [8192, 1024], P('leaf', 'head')
- leaf_value_grad: bfloat16 [8192, 1024], P('leaf', 'head')
The draws below stay inside these ranges and needn't reach their ends.
Inputs may be any that keep to these rules, and one draw needn't show every extreme that they name: `branch_lengths`: some branch has all 512 tokens live. `leaf_lengths`: some leaf has all 128 tokens live.
All inputs are finite; a program needn't handle non-finite values. No bound on the sum of `leaf_lengths` on one device may be relied on, other than what follows from the above.
Results may differ from the reference program's by a relative error of at most 0.013.
Values may be sent and summed in bfloat16 or wider, within the bound.
No kernel may reach another device: no remote copies, remote signals or barrier semaphores. Data moves between devices by JAX's collectives and lax.ppermute only.
A program may use at most 128 MiB of HBM per device.

```python
import math
import jax
import jax.numpy as jnp
import numpy as np
from jax import lax

HEADS = 64
KV_HEADS = 8
HEAD_DIM = 128
GROUP = 8
LEAF_LEN = 128
BRANCH_DEV = 64
ROOT_DEV = 4
LEAVES = 64
BRANCHES = 8
BRANCH_LEN = 512
ROOT = 1024
N_LEAF = 64
N_HEAD = 4


def draw_leaf_key(key, part):
    key = jax.random.fold_in(key, 3)
    rows = LEAVES * LEAF_LEN
    base = jnp.clip(jax.random.normal(key, (rows, KV_HEADS * HEAD_DIM), jnp.float32), -6.0, 6.0)
    return base.astype(jnp.bfloat16)


def draw_leaf_query(key, part):
    key = jax.random.fold_in(key, 5)
    rows = LEAVES * LEAF_LEN
    base = jnp.clip(jax.random.normal(key, (rows, HEADS * HEAD_DIM), jnp.float32), -6.0, 6.0)
    return base.astype(jnp.bfloat16)


def steps_of(stream_key, shape, shards, least, top_value):
    factor_of = 1.0
    for position, parts in shards:
        heights = jax.random.uniform(jax.random.fold_in(jax.random.fold_in(stream_key, 6), position), (parts,), jnp.float32, least / len(shards), top_value / len(shards))
        factor_of = factor_of * jnp.repeat(jnp.exp(heights), shape[position] // parts).reshape((-1,) + (1,) * (len(shape) - 1 - position))
    return factor_of


def profile(number_of, total, bound, skew):
    portions = [(1 << 20) // math.isqrt(standing ** skew) + 1 for standing in range(2, number_of + 1)]
    surplus, counts = total - bound - (number_of - 1), [1] * (number_of - 1)
    while surplus > 0:
        candidates = [i for i in range(number_of - 1) if counts[i] < bound]
        pool, budget = sum([portions[i] for i in candidates]), surplus
        for i in candidates:
            addition = min(bound - counts[i], max(1, budget * portions[i] // pool), surplus)
            counts[i] = counts[i] + addition
            surplus = surplus - addition
    return np.array([bound] + counts)


def ragged(stream_key, number_of, total, most, skew):
    if number_of == 2:
        one = jax.random.randint(stream_key, (), max(1, total - most), min(most, total - 1) + 1)
        return jnp.stack([one, total - one])
    tallies = jnp.asarray(profile(number_of, total, most, skew), jnp.int32)
    twos = (number_of - 1) // 2
    donor, receiver = tallies[1:1 + 2 * twos:2], tallies[2:2 + 2 * twos:2]
    margin = jnp.minimum(donor - 1, most - receiver)
    shifted = jax.random.randint(jax.random.fold_in(stream_key, 1), (twos,), 0, 1 << 20) % (margin + 1)
    tallies = tallies.at[1:1 + 2 * twos:2].set(donor - shifted).at[2:2 + 2 * twos:2].set(receiver + shifted)
    return tallies[jax.random.permutation(jax.random.fold_in(stream_key, 2), number_of)]


def normal_values(key, shape, scale, bound, shards=(), kind=jnp.bfloat16):
    entries = jax.random.normal(key, shape, jnp.float32) * scale
    if len(shards) > 0:
        entries = steps_of(key, shape, shards, -0.22, 0.18) * entries
    return jnp.clip(entries, min=-bound, max=bound).astype(kind)


def setup_inputs(seed: int = 0) -> dict:
    arg_keys = jax.random.split(jax.random.key(seed), 15)
    root_query = normal_values(arg_keys[0], (ROOT, HEADS * HEAD_DIM), 1.0, 6.0, ((0, 64), (1, 4)))
    branch_query = normal_values(arg_keys[1], (BRANCHES * BRANCH_LEN, HEADS * HEAD_DIM), 1.0, 6.0, ((0, 64), (1, 4)))
    leaf_query = draw_leaf_query(jax.random.fold_in(arg_keys[14], 71), 0)
    root_key = normal_values(arg_keys[3], (ROOT, KV_HEADS * HEAD_DIM), 1.0, 6.0, ((0, 256),))
    root_value = normal_values(arg_keys[4], (ROOT, KV_HEADS * HEAD_DIM), 1.0, 6.0, ((0, 256),))
    branch_key = normal_values(arg_keys[5], (BRANCHES * BRANCH_LEN, KV_HEADS * HEAD_DIM), 1.0, 6.0, ((0, 64), (1, 4)))
    branch_value = normal_values(arg_keys[6], (BRANCHES * BRANCH_LEN, KV_HEADS * HEAD_DIM), 1.0, 6.0, ((0, 64), (1, 4)))
    leaf_key = draw_leaf_key(jax.random.fold_in(arg_keys[14], 71), 0)
    leaf_value = normal_values(arg_keys[8], (LEAVES * LEAF_LEN, KV_HEADS * HEAD_DIM), 1.0, 6.0, ((0, 64), (1, 4)))
    root_grad_out = normal_values(arg_keys[9], (ROOT, HEADS * HEAD_DIM), 1.0, 6.0, ((0, 64), (1, 4)))
    branch_grad_out = normal_values(arg_keys[10], (BRANCHES * BRANCH_LEN, HEADS * HEAD_DIM), 1.0, 6.0, ((0, 64), (1, 4)))
    leaf_grad_out = normal_values(arg_keys[11], (LEAVES * LEAF_LEN, HEADS * HEAD_DIM), 1.0, 6.0, ((0, 64), (1, 4)))
    branch_lengths = ragged(arg_keys[12], BRANCHES, BRANCH_LEN + (BRANCHES - 1) * BRANCH_LEN * 2 // 3, BRANCH_LEN, 1).astype(jnp.int32)
    leaf_lengths = ragged(arg_keys[13], LEAVES, LEAF_LEN + (LEAVES - 1) * LEAF_LEN * 2 // 3, LEAF_LEN, 1).astype(jnp.int32)
    return {"root_query": root_query, "branch_query": branch_query, "leaf_query": leaf_query, "root_key": root_key, "root_value": root_value, "branch_key": branch_key, "branch_value": branch_value, "leaf_key": leaf_key, "leaf_value": leaf_value, "root_grad_out": root_grad_out, "branch_grad_out": branch_grad_out, "leaf_grad_out": leaf_grad_out, "branch_lengths": branch_lengths, "leaf_lengths": leaf_lengths}


def tree_mask(root_place, branch_place, branch_live, leaf_live, root_count, branch_count, leaf_count):
    query_kind = jnp.concatenate([jnp.zeros(root_place.shape, jnp.int32), jnp.ones(branch_place.shape, jnp.int32), jnp.full((leaf_count,), 2, jnp.int32)])
    query_place = jnp.concatenate([root_place, branch_place, jnp.arange(leaf_count, dtype=jnp.int32)])
    key_kind = jnp.concatenate([jnp.zeros((root_count,), jnp.int32), jnp.ones((branch_count,), jnp.int32), jnp.full((leaf_count,), 2, jnp.int32)])
    key_place = jnp.concatenate([jnp.arange(root_count, dtype=jnp.int32), jnp.arange(branch_count, dtype=jnp.int32), jnp.arange(leaf_count, dtype=jnp.int32)])
    row_kind = query_kind[:, None]
    row_place = query_place[:, None]
    col_kind = key_kind[None, :]
    col_place = key_place[None, :]
    causal = col_place <= row_place
    from_root = (col_kind == 0) & ((row_kind > 0) | causal)
    from_branch = (col_kind == 1) & (row_kind > 0) & (col_place < branch_live) & ((row_kind == 2) | causal)
    from_leaf = (col_kind == 2) & (row_kind == 2) & (col_place < leaf_live) & causal
    allowed = from_root | from_branch | from_leaf
    live = (query_kind == 0) | (query_kind == 1) & (query_place < branch_live) | (query_kind == 2) & (query_place < leaf_live)
    return (allowed, live)

def group_terms(query, key, value, grad, allowed):
    scale = 1.0 / math.sqrt(query.shape[-1])
    query_f = query.astype(jnp.float32)
    key_f = key.astype(jnp.float32)
    value_f = value.astype(jnp.float32)
    grad_f = grad.astype(jnp.float32)
    scores = jnp.einsum('qgd,nd->gqn', query_f, key_f) * scale
    scores = jnp.where(allowed[None], scores, -jnp.inf)
    top = lax.optimization_barrier(jnp.max(scores, axis=-1, keepdims=True))
    expo = jnp.exp(scores - top)
    weights = expo / lax.optimization_barrier(jnp.sum(expo, axis=-1, keepdims=True))
    rounded = lax.optimization_barrier(weights.astype(jnp.bfloat16)).astype(jnp.float32)
    attended = jnp.einsum('gqn,nd->qgd', rounded, value_f)
    weight_grad = jnp.einsum('qgd,nd->gqn', grad_f, value_f)
    delta = lax.optimization_barrier(jnp.sum(weights * weight_grad, axis=-1, keepdims=True))
    score_grad = lax.optimization_barrier((weights * (weight_grad - delta) * scale).astype(jnp.bfloat16)).astype(jnp.float32)
    query_grad = jnp.einsum('gqn,nd->qgd', score_grad, key_f)
    key_grad = jnp.einsum('gqn,qgd->nd', score_grad, query_f)
    value_grad = jnp.einsum('gqn,qgd->nd', rounded, grad_f)
    return (attended, query_grad, key_grad, value_grad)

def all_heads(queries, keys, values, grads, allowed, live):
    masked = jnp.where(live[:, None], grads, jnp.zeros_like(grads))
    live_rows = live.astype(jnp.float32)[:, None]
    kv_count = keys.shape[1] // HEAD_DIM
    per_group = queries.shape[1] // kv_count
    rows = queries.shape[0]
    outs_a, outs_q, outs_k, outs_v = ([], [], [], [])
    for index in range(kv_count):
        query = queries[:, index * per_group:(index + 1) * per_group].reshape(rows, -1, HEAD_DIM)
        grad = masked[:, index * per_group:(index + 1) * per_group].reshape(rows, -1, HEAD_DIM)
        key = keys[:, index * HEAD_DIM:(index + 1) * HEAD_DIM]
        value = values[:, index * HEAD_DIM:(index + 1) * HEAD_DIM]
        attended, query_grad, key_grad, value_grad = group_terms(query, key, value, grad, allowed)
        outs_a.append(attended.reshape(rows, per_group))
        outs_q.append(query_grad.reshape(rows, per_group))
        outs_k.append(key_grad)
        outs_v.append(value_grad)
    attended = (jnp.concatenate(outs_a, 1) * live_rows).astype(jnp.bfloat16)
    query_grad = jnp.concatenate(outs_q, 1).astype(jnp.bfloat16)
    return (attended, query_grad, jnp.concatenate(outs_k, 1), jnp.concatenate(outs_v, 1))

def reference(root_query, branch_query, leaf_query, root_key, root_value, branch_key, branch_value, leaf_key, leaf_value, root_grad_out, branch_grad_out, leaf_grad_out, branch_lengths, leaf_lengths):
    root_share = ROOT_DEV * N_HEAD
    kv_width = root_key.shape[1]

    def rows(array, start, count):
        return lax.dynamic_slice_in_dim(array, start, count, 0)

    def one_leaf(carry, leaf_index):
        root_key_sum, root_value_sum, branch_key_sum, branch_value_sum = carry
        branch_index = leaf_index // GROUP
        within = leaf_index % GROUP
        root_start = leaf_index * root_share
        branch_base = branch_index * BRANCH_LEN
        branch_start = branch_base + within * BRANCH_DEV
        leaf_start = leaf_index * LEAF_LEN
        queries = jnp.concatenate([rows(root_query, root_start, root_share), rows(branch_query, branch_start, BRANCH_DEV), rows(leaf_query, leaf_start, LEAF_LEN)], 0)
        grads = jnp.concatenate([rows(root_grad_out, root_start, root_share), rows(branch_grad_out, branch_start, BRANCH_DEV), rows(leaf_grad_out, leaf_start, LEAF_LEN)], 0)
        keys = jnp.concatenate([root_key, rows(branch_key, branch_base, BRANCH_LEN), rows(leaf_key, leaf_start, LEAF_LEN)], 0)
        values = jnp.concatenate([root_value, rows(branch_value, branch_base, BRANCH_LEN), rows(leaf_value, leaf_start, LEAF_LEN)], 0)
        root_place = (root_start + jnp.arange(root_share, dtype=jnp.int32)).astype(jnp.int32)
        branch_place = (within * BRANCH_DEV + jnp.arange(BRANCH_DEV, dtype=jnp.int32)).astype(jnp.int32)
        allowed, live = tree_mask(root_place, branch_place, branch_lengths[branch_index], leaf_lengths[leaf_index], ROOT, BRANCH_LEN, LEAF_LEN)
        attended, query_grad, key_grad, value_grad = all_heads(queries, keys, values, grads, allowed, live)
        root_key_sum = root_key_sum + key_grad[:ROOT]
        root_value_sum = root_value_sum + value_grad[:ROOT]
        branch_key_sum = lax.dynamic_update_slice_in_dim(branch_key_sum, rows(branch_key_sum, branch_base, BRANCH_LEN) + key_grad[ROOT:ROOT + BRANCH_LEN], branch_base, 0)
        branch_value_sum = lax.dynamic_update_slice_in_dim(branch_value_sum, rows(branch_value_sum, branch_base, BRANCH_LEN) + value_grad[ROOT:ROOT + BRANCH_LEN], branch_base, 0)
        middle = root_share + BRANCH_DEV
        outputs = (attended[:root_share], attended[root_share:middle], attended[middle:], query_grad[:root_share], query_grad[root_share:middle], query_grad[middle:], key_grad[ROOT + BRANCH_LEN:].astype(jnp.bfloat16), value_grad[ROOT + BRANCH_LEN:].astype(jnp.bfloat16))
        return ((root_key_sum, root_value_sum, branch_key_sum, branch_value_sum), outputs)
    start = (jnp.zeros((ROOT, kv_width), jnp.float32), jnp.zeros((ROOT, kv_width), jnp.float32), jnp.zeros((BRANCHES * BRANCH_LEN, kv_width), jnp.float32), jnp.zeros((BRANCHES * BRANCH_LEN, kv_width), jnp.float32))
    sums, outputs = lax.scan(one_leaf, start, jnp.arange(N_LEAF, dtype=jnp.int32))
    flat = [piece.reshape(-1, piece.shape[-1]) for piece in outputs]
    return (flat[0], flat[1], flat[2], flat[3], flat[4], flat[5], sums[0].astype(jnp.bfloat16), sums[1].astype(jnp.bfloat16), sums[2].astype(jnp.bfloat16), sums[3].astype(jnp.bfloat16), flat[6], flat[7])
```

```python
import functools, math
import jax, jax.numpy as jnp
from jax import lax
from jax.experimental import pallas as pl
from jax.experimental.pallas import tpu as pltpu
from jax.sharding import Mesh, PartitionSpec as P

D = 128
HG = 8
GROUP = 8
ROOT, BRANCH, LEAF = 1024, 512, 128
KEYS = ROOT + BRANCH + LEAF
NEG = -1e30
bf16, f32, i32 = jnp.bfloat16, jnp.float32, jnp.int32
SCALE = 1.0 / math.sqrt(D)
C2 = SCALE * math.log2(math.e)
NT = (((1,), (1,)), ((), ()))
NN = (((1,), (0,)), ((), ()))
CH = 256


def dot(a, b, dims=NN):
    return lax.dot_general(a, b, dims, preferred_element_type=f32)


def chunks(n):
    return [(a, min(CH, n - a)) for a in range(0, n, CH)]


def attend_kernel(place, rq, bq, lq, rg, bg, lg, r0, r1, r2, r3, b0, b1, lk, lv, *rest):
    (ra, ba, la, rdq, bdq, ldq, ldk, ldv, r0o, r1o, r2o, r3o, b0o, b1o,
     kk, vv, kt, vt, ss, dd, ak, av) = rest[-22:]
    y, x, z = place[0], place[1], place[2]
    branch_live, leaf_live = place[3], place[4]
    within = (x & 1) * 4 + z
    leaf_index = y * 16 + x * 4 + z
    for i, r in enumerate((r0, r1, r2, r3)):
        kk[i * 256:(i + 1) * 256, :] = r[:, :D]
        vv[i * 256:(i + 1) * 256, :] = r[:, D:]
    for i, r in enumerate((b0, b1)):
        kk[ROOT + i * 256:ROOT + (i + 1) * 256, :] = r[:, :D]
        vv[ROOT + i * 256:ROOT + (i + 1) * 256, :] = r[:, D:]
    kk[ROOT + BRANCH:, :] = lk[...]
    vv[ROOT + BRANCH:, :] = lv[...]
    for a, n in chunks(KEYS):
        kt[:, a:a + n] = kk[a:a + n, :].astype(f32).T.astype(bf16)
        vt[:, a:a + n] = vv[a:a + n, :].astype(f32).T.astype(bf16)
    ak[...] = jnp.zeros_like(ak)
    av[...] = jnp.zeros_like(av)

    def root_pos(a, n, N):
        r = lax.broadcasted_iota(i32, (n, N), 0) + a
        return (((y - (r >> 8)) & 3) << 8) | (((x - (r >> 6)) & 3) << 6) | (r & 63)

    def branch_pos(a, n, N):
        r = lax.broadcasted_iota(i32, (n, N), 0) + a
        return (((x ^ (r >> 8)) & 1) << 8) | (((z - (r >> 6)) & 3) << 6) | (r & 63)

    def tile(q, do, nk, tok, live_col, mask):
        N = q.shape[0]
        m = jnp.full((1, N), NEG, f32)
        for a, n in chunks(nk):
            s = dot(kk[a:a + n, :], q, NT) * C2
            ok = mask(a, n, N)
            if ok is not None:
                s = jnp.where(ok, s, NEG)
            ss[a:a + n, :N] = s
            m = jnp.maximum(m, jnp.max(s, axis=0, keepdims=True))
            dd[a:a + n, :N] = dot(vv[a:a + n, :], do, NT)
        l = jnp.zeros((1, N), f32)
        dl = jnp.zeros((1, N), f32)
        for a, n in chunks(nk):
            e = jnp.exp2(ss[a:a + n, :N] - m)
            ss[a:a + n, :N] = e
            l = l + jnp.sum(e, axis=0, keepdims=True)
            dl = dl + jnp.sum(e * dd[a:a + n, :N], axis=0, keepdims=True)
        inv = 1.0 / l
        delta = dl * inv
        ot = jnp.zeros((D, N), f32)
        qt = jnp.zeros((D, N), f32)
        for a, n in chunks(nk):
            w = ss[a:a + n, :N] * inv
            p = w.astype(bf16)
            ds = (w * (dd[a:a + n, :N] - delta)).astype(bf16)
            av[a:a + n, :] += dot(p, do)
            ak[a:a + n, :] += dot(ds, q)
            ot = ot + dot(vt[:, a:a + n], p)
            qt = qt + dot(kt[:, a:a + n], ds)
        o = jnp.where(live_col, ot, 0.0).T.astype(bf16)
        dq = (qt * SCALE).T.astype(bf16)
        return o, dq

    def grab(ref, heads):
        return jnp.concatenate([ref[:, h] for h in heads], axis=0)

    def leaf_mask(a, n, N):
        if a < ROOT:
            return None
        if a < ROOT + BRANCH:
            return branch_pos(a - ROOT, n, N) < branch_live
        k = lax.broadcasted_iota(i32, (n, N), 0)
        t = lax.broadcasted_iota(i32, (n, N), 1) & (LEAF - 1)
        return (k < leaf_live) & (k <= t)

    def leaf_body(i, c):
        hs = [pl.ds(pl.multiple_of((2 * i + j) * D, D), D) for j in range(2)]
        tok = lax.broadcasted_iota(i32, (2 * LEAF, 1), 0) & (LEAF - 1)
        q = grab(lq, hs)
        do = jnp.where(tok < leaf_live, grab(lg, hs), jnp.zeros((), bf16))
        col = lax.broadcasted_iota(i32, (1, 2 * LEAF), 1) & (LEAF - 1)
        o, dq = tile(q, do, KEYS, tok, col < leaf_live, leaf_mask)
        for j, h in enumerate(hs):
            la[:, h] = o[j * LEAF:(j + 1) * LEAF]
            ldq[:, h] = dq[j * LEAF:(j + 1) * LEAF]
        return c
    lax.fori_loop(0, HG // 2, leaf_body, 0)

    BT = 64
    def branch_mask(a, n, N):
        if a < ROOT:
            return None
        p = branch_pos(a - ROOT, n, N)
        t = (lax.broadcasted_iota(i32, (n, N), 1) & (BT - 1)) + within * BT
        return (p < branch_live) & (p <= t)

    def branch_body(i, c):
        hs = [pl.ds(pl.multiple_of((4 * i + j) * D, D), D) for j in range(4)]
        tok = (lax.broadcasted_iota(i32, (4 * BT, 1), 0) & (BT - 1)) + within * BT
        q = grab(bq, hs)
        do = jnp.where(tok < branch_live, grab(bg, hs), jnp.zeros((), bf16))
        col = (lax.broadcasted_iota(i32, (1, 4 * BT), 1) & (BT - 1)) + within * BT
        o, dq = tile(q, do, ROOT + BRANCH, tok, col < branch_live, branch_mask)
        for j, h in enumerate(hs):
            ba[:, h] = o[j * BT:(j + 1) * BT]
            bdq[:, h] = dq[j * BT:(j + 1) * BT]
        return c
    lax.fori_loop(0, HG // 4, branch_body, 0)

    RT = 16
    def root_mask(a, n, N):
        t = (lax.broadcasted_iota(i32, (n, N), 1) & (RT - 1)) + leaf_index * RT
        return root_pos(a, n, N) <= t
    hs = [pl.ds(j * D, D) for j in range(HG)]
    q = grab(rq, hs)
    do = grab(rg, hs)
    o, dq = tile(q, do, ROOT, None, lax.broadcasted_iota(i32, (1, HG * RT), 1) >= 0, root_mask)
    for j, h in enumerate(hs):
        ra[:, h] = o[j * RT:(j + 1) * RT]
        rdq[:, h] = dq[j * RT:(j + 1) * RT]

    for i, r in enumerate((r0o, r1o, r2o, r3o)):
        s = slice(i * 256, (i + 1) * 256)
        r[:, :D] = (ak[s, :] * SCALE).astype(r.dtype)
        r[:, D:] = av[s, :].astype(r.dtype)
    for i, r in enumerate((b0o, b1o)):
        s = slice(ROOT + i * 256, ROOT + (i + 1) * 256)
        r[:, :D] = (ak[s, :] * SCALE).astype(r.dtype)
        r[:, D:] = av[s, :].astype(r.dtype)
    ldk[...] = (ak[ROOT + BRANCH:, :] * SCALE).astype(bf16)
    ldv[...] = av[ROOT + BRANCH:, :].astype(bf16)


def attend(g, place, queries, grads, roots, branch, lk, lv, prev=None):
    W = HG * D
    def col(rows, w):
        return pl.BlockSpec((rows, w), lambda i: (0, g))
    def whole(shape):
        return pl.BlockSpec(shape, lambda i: (0, 0))
    in_specs = [pl.BlockSpec(memory_space=pltpu.SMEM)]
    in_specs += [col(n, W) for n in (16, 64, 128)] * 2
    in_specs += [whole((256, 2 * D))] * 4 + [col(256, 2 * D)] * 2
    in_specs += [col(LEAF, D)] * 2
    args = [place, *queries, *grads, *roots, *branch, lk, lv]
    alias = {}
    if prev is not None:
        for i, p in enumerate(prev):
            alias[len(args)] = i
            args.append(p)
            in_specs.append(pl.BlockSpec(memory_space=pl.ANY))
    S = jax.ShapeDtypeStruct
    outs = [S((n, 2 * W), bf16) for n in (16, 64, 128)] * 2 + [S((LEAF, 2 * D), bf16)] * 2
    out_specs = [col(n, W) for n in (16, 64, 128)] * 2 + [col(LEAF, D)] * 2
    outs += [S((256, 2 * D), f32)] + [S((256, 2 * D), bf16)] * 3
    out_specs += [whole((256, 2 * D))] * 4
    outs += [S((256, 2 * D), f32), S((256, 2 * D), bf16)]
    out_specs += [whole((256, 2 * D))] * 2
    scratch = [pltpu.VMEM((KEYS, D), bf16)] * 2 + [pltpu.VMEM((D, KEYS), bf16)] * 2
    scratch += [pltpu.VMEM((KEYS, 256), f32)] * 2 + [pltpu.VMEM((KEYS, D), f32)] * 2
    return pl.pallas_call(
        attend_kernel, grid=(1,), out_shape=outs, in_specs=in_specs, out_specs=out_specs,
        scratch_shapes=scratch, input_output_aliases=alias,
        compiler_params=pltpu.CompilerParams(vmem_limit_bytes=40 * 2**20),
        cost_estimate=pl.CostEstimate(flops=2 * 6 * 1664 * 1664 * 128, bytes_accessed=6 * 2**20, transcendentals=1664 * 1664),
        name="attend",
    )(*args)


def split_rows(r0, r1, r2, r3, o0, o1):
    n = r0.shape[0]
    for i, r in enumerate((r0, r1, r2, r3)):
        o0[i * n:(i + 1) * n, :] = r[:, :2 * D]
        o1[i * n:(i + 1) * n, :] = r[:, 2 * D:]


def stack_rows(r0, r1, r2, r3, o):
    n = r0.shape[0]
    for i, r in enumerate((r0, r1, r2, r3)):
        o[i * n:(i + 1) * n, :] = r[...]


def add_y(own0, a1, a2, a3, own1, c1, c2, c3, o0, o1, o2, o3):
    n = own0.shape[0] // 4
    for j, (own, *parts) in enumerate(((own0, a1, a2, a3), (own1, c1, c2, c3))):
        for i, o in enumerate((o0, o1, o2, o3)):
            s = slice(i * n, (i + 1) * n)
            t = own[s, :]
            for p in parts:
                t = t + p[s, :].astype(f32)
            o[:, j * 2 * D:(j + 1) * 2 * D] = t.astype(o.dtype)


def add_pair(own0, a1, own1, c1, o0, o1, o2, o3):
    n = own0.shape[0] // 4
    for j, (own, p) in enumerate(((own0, a1), (own1, c1))):
        for i, o in enumerate((o0, o1, o2, o3)):
            s = slice(i * n, (i + 1) * n)
            o[:, j * 2 * D:(j + 1) * 2 * D] = (own[s, :] + p[s, :].astype(f32)).astype(o.dtype)


def add_x(own, a1, a2, a3, o):
    o[...] = own[...] + a1[...].astype(f32) + a2[...].astype(f32) + a3[...].astype(f32)


def add_z(own, a1, a2, a3, ok, ov):
    t = own[...] + a1[...].astype(f32) + a2[...].astype(f32) + a3[...].astype(f32)
    for g in range(2):
        ok[:, g * D:(g + 1) * D] = t[:, 2 * g * D:(2 * g + 1) * D].astype(ok.dtype)
        ov[:, g * D:(g + 1) * D] = t[:, (2 * g + 1) * D:(2 * g + 2) * D].astype(ov.dtype)


def small(body, outs, *args):
    return pl.pallas_call(
        body,
        out_shape=[jax.ShapeDtypeStruct(s, t) for s, t in outs],
        in_specs=[pl.BlockSpec(memory_space=pltpu.VMEM)] * len(args),
        out_specs=[pl.BlockSpec(memory_space=pltpu.VMEM)] * len(outs),
        cost_estimate=pl.CostEstimate(flops=10**6, bytes_accessed=2**20, transcendentals=0),
    )(*args)


def shift(a, axis, d):
    return lax.ppermute(a, axis, [(i, (i + d) % 4) for i in range(4)])


def shifts(a, axis):
    return [shift(a, axis, d) for d in (1, 2, 3)]


def back(parts, axis):
    return [shift(p, axis, -d) for d, p in zip((1, 2, 3), parts)]


def pair(a):
    return lax.ppermute(a, "x", [(i, i ^ 1) for i in range(4)])


def local(
    root_query, branch_query, leaf_query, root_key, root_value, branch_key, branch_value,
    leaf_key, leaf_value, root_grad_out, branch_grad_out, leaf_grad_out,
    branch_lengths, leaf_lengths,
):
    y, x, z = (lax.axis_index(a) for a in ("y", "x", "z"))
    branch_live = branch_lengths[(y * 16 + x * 4 + z) // GROUP]
    place = jnp.stack([y, x, z, branch_live, leaf_lengths[0]]).astype(i32)
    queries = (root_query, branch_query, leaf_query)
    grads = (root_grad_out, branch_grad_out, leaf_grad_out)

    raw = jnp.stack([root_key.reshape(4, 4, 2, D), root_value.reshape(4, 4, 2, D)], 3)
    raw = raw.reshape(4, 4, 4 * D).transpose(1, 0, 2)
    raw = jnp.broadcast_to(raw[None], (4, 4, 4, 4 * D)).reshape(16, 4, 4 * D)
    own = lax.all_to_all(raw, ("z", "head"), 0, 0, tiled=True).reshape(64, 4 * D)
    r0, r1 = small(split_rows, [((256, 2 * D), bf16)] * 2, own, *shifts(own, "x"))

    mine = jnp.stack([branch_key.reshape(64, 2, D), branch_value.reshape(64, 2, D)], 2)
    mine = mine.reshape(64, 4 * D)
    b_own, = small(stack_rows, [((256, 4 * D), bf16)], mine, *shifts(mine, "z"))
    branch = (b_own, pair(b_own))

    roots0 = [r0, *shifts(r0, "y")]
    r1, *roots0 = lax.optimization_barrier((r1, *roots0))
    roots1 = [r1, *shifts(r1, "y")]

    first = attend(0, place, queries, grads, roots0, branch, leaf_key, leaf_value)
    ry0 = back(first[9:12], "y")
    bx0 = pair(first[13])
    second = attend(1, place, queries, grads, roots1, branch, leaf_key, leaf_value, first[:8])
    y1, b1, *rest = lax.optimization_barrier((second[9:12], second[13], *ry0, bx0))
    ry0, bx0 = rest[:3], rest[3]
    ry1 = back(y1, "y")
    bx1 = pair(b1)
    own, *parts = small(
        add_y, [((64, 4 * D), f32)] + [((64, 4 * D), bf16)] * 3,
        first[8], *ry0, second[8], *ry1,
    )
    sums, = small(add_x, [((64, 4 * D), f32)], own, *back(parts, "x"))
    own, *parts = small(
        add_pair, [((64, 4 * D), f32)] + [((64, 4 * D), bf16)] * 3,
        first[12], bx0, second[12], bx1,
    )
    bk, bv = small(add_z, [((64, 2 * D), bf16)] * 2, own, *back(parts, "z"))
    last = lax.all_to_all(sums.reshape(16, 4, 4 * D), ("z", "head"), 0, 0, tiled=True)
    last = jnp.sum(last.reshape(4, 4, 4, 2, 2, D), 0).astype(bf16)
    rk = last[:, :, :, 0].transpose(1, 0, 2, 3).reshape(4, 8 * D)
    rv = last[:, :, :, 1].transpose(1, 0, 2, 3).reshape(4, 8 * D)
    ra, ba, la, rdq, bdq, ldq, ldk, ldv = second[:8]
    return ra, ba, la, rdq, bdq, ldq, rk, rv, bk, bv, ldk, ldv


def solution(mesh):
    fine = Mesh(mesh.devices.reshape(4, 4, 4, 4), ("y", "x", "z", "head"))
    leaf = ("y", "x", "z")
    both, rows = P(leaf, "head"), P((*leaf, "head"), None)
    return jax.shard_map(
        local,
        mesh=fine,
        in_specs=(both, both, both, rows, rows, both, both, both, both, both, both, both, P(), P(leaf)),
        out_specs=(both, both, both, both, both, both, rows, rows, both, both, both, both),
        check_vma=False,
    )
```

```python
import functools, math
import jax, jax.numpy as jnp
from jax import lax
from jax.experimental import pallas as pl
from jax.experimental.pallas import tpu as pltpu
from jax.sharding import Mesh, PartitionSpec as P

D = 128
HG = 8
GROUP = 8
ROOT, BRANCH, LEAF = 1024, 512, 128
KEYS = ROOT + BRANCH + LEAF
NEG = -1e30
bf16, f32, i32 = jnp.bfloat16, jnp.float32, jnp.int32
SCALE = 1.0 / math.sqrt(D)
C2 = SCALE * math.log2(math.e)
NT = (((1,), (1,)), ((), ()))
NN = (((1,), (0,)), ((), ()))
CH = 256


def dot(a, b, dims=NN):
    return lax.dot_general(a, b, dims, preferred_element_type=f32)


def chunks(n):
    return [(a, min(CH, n - a)) for a in range(0, n, CH)]


def attend_kernel(where, g, branch_lengths, leaf_lengths, *rest):
    far_in, (r0, r1, r2, r3, b0, b1) = rest[:8], rest[8:14]
    rest = rest[-40:]
    far_out, (r0o, r1o, r2o, r3o, b0o, b1o) = rest[:8], rest[8:14]
    near_in, near_out = rest[14:22], rest[22:30]
    kk, vv, kt, vt, ss, dd, ak, av, sem_in, sem_out = rest[30:]
    rq, bq, lq, rg, bg, lg, lk, lv = near_in
    ra, ba, la, rdq, bdq, ldq, ldk, ldv = near_out

    def columns(ref, width):
        return ref.at[:, pl.ds(g * width, width)]

    loads = [pltpu.make_async_copy(columns(f, n.shape[1]), n, sem_in.at[i])
             for i, (f, n) in enumerate(zip(far_in, near_in))]
    stores = [pltpu.make_async_copy(n, columns(f, n.shape[1]), sem_out.at[i])
              for i, (f, n) in enumerate(zip(far_out, near_out))]
    for i in (6, 7, 2, 5, 1, 4, 0, 3):
        loads[i].start()
    y, x, z = where()
    within = (x & 1) * 4 + z
    leaf_index = y * 16 + x * 4 + z
    branch_live, leaf_live = branch_lengths[leaf_index // GROUP], leaf_lengths[0]
    def rows_at(n, start):
        return pl.ds(pl.multiple_of(start, n), n)
    root_rows = [rows_at(256, ((y - i) & 3) * 256) for i in range(4)]
    branch_rows = [rows_at(256, ROOT + ((x ^ i) & 1) * 256) for i in range(2)]
    for s, r in zip(root_rows + branch_rows, (r0, r1, r2, r3, b0, b1)):
        kk[s, :] = r[:, :D]
        vv[s, :] = r[:, D:]
    loads[6].wait()
    loads[7].wait()
    kk[ROOT + BRANCH:, :] = lk[...]
    vv[ROOT + BRANCH:, :] = lv[...]
    for a, n in chunks(KEYS):
        kt[:, a:a + n] = kk[a:a + n, :].astype(f32).T.astype(bf16)
        vt[:, a:a + n] = vv[a:a + n, :].astype(f32).T.astype(bf16)
    ak[...] = jnp.zeros_like(ak)
    av[...] = jnp.zeros_like(av)

    class Tile:
        def __init__(self, slot, q, do, nk, live, mask, done):
            self.q, self.do, self.nk, self.live, self.mask, self.done = q, do, nk, live, mask, done
            self.N = q.shape[0]
            self.ss, self.dd = ss.at[slot], dd.at[slot]
            self.m = jnp.full((1, self.N), NEG, f32)
            self.l = jnp.zeros((1, self.N), f32)
            self.dl = jnp.zeros((1, self.N), f32)
            self.ot = jnp.zeros((D, self.N), f32)
            self.qt = jnp.zeros((D, self.N), f32)

        def score(self, a, n):
            s = dot(kk[a:a + n, :], self.q, NT) * C2
            ok = self.mask(a, n, self.N)
            if ok is not None:
                s = jnp.where(ok, s, NEG)
            self.ss[a:a + n, :self.N] = s
            self.m = jnp.maximum(self.m, jnp.max(s, axis=0, keepdims=True))
            self.dd[a:a + n, :self.N] = dot(vv[a:a + n, :], self.do, NT)

        def weigh(self, a, n):
            e = jnp.exp2(self.ss[a:a + n, :self.N] - self.m)
            self.ss[a:a + n, :self.N] = e
            self.l = self.l + jnp.sum(e, axis=0, keepdims=True)
            self.dl = self.dl + jnp.sum(e * self.dd[a:a + n, :self.N], axis=0, keepdims=True)

        def norm(self):
            self.inv = 1.0 / self.l
            self.delta = self.dl * self.inv

        def spread(self, a, n):
            w = self.ss[a:a + n, :self.N] * self.inv
            p = w.astype(bf16)
            ds = (w * (self.dd[a:a + n, :self.N] - self.delta)).astype(bf16)
            av[a:a + n, :] += dot(p, self.do)
            ak[a:a + n, :] += dot(ds, self.q)
            self.ot = self.ot + dot(vt[:, a:a + n], p)
            self.qt = self.qt + dot(kt[:, a:a + n], ds)

        def finish(self):
            o = jnp.where(self.live, self.ot, 0.0).T.astype(bf16)
            self.done(o, (self.qt * SCALE).T.astype(bf16))

    def grab(ref, heads):
        return jnp.concatenate([ref[:, h] for h in heads], axis=0)

    def leaf_mask(a, n, N):
        if a < ROOT:
            return None
        if a < ROOT + BRANCH:
            return lax.broadcasted_iota(i32, (n, N), 0) + (a - ROOT) < branch_live
        k = lax.broadcasted_iota(i32, (n, N), 0)
        t = lax.broadcasted_iota(i32, (n, N), 1) & (LEAF - 1)
        return (k < leaf_live) & (k <= t)

    def writer(heads, T, o_ref, dq_ref, sent):
        def done(o, dq):
            for j, h in enumerate(heads):
                o_ref[:, h] = o[j * T:(j + 1) * T]
                dq_ref[:, h] = dq[j * T:(j + 1) * T]
            for i in sent:
                stores[i].start()
        return done

    def leaf_tile(i):
        def make(slot):
            if i == 0:
                loads[2].wait()
                loads[5].wait()
            hs = [slice((2 * i + j) * D, (2 * i + j + 1) * D) for j in range(2)]
            tok = lax.broadcasted_iota(i32, (2 * LEAF, 1), 0) & (LEAF - 1)
            do = jnp.where(tok < leaf_live, grab(lg, hs), jnp.zeros((), bf16))
            col = lax.broadcasted_iota(i32, (1, 2 * LEAF), 1) & (LEAF - 1)
            done = writer(hs, LEAF, la, ldq, (2, 5) if i == 3 else ())
            return Tile(slot, grab(lq, hs), do, KEYS, col < leaf_live, leaf_mask, done)
        return make

    BT = 64
    def branch_mask(a, n, N):
        if a < ROOT:
            return None
        p = lax.broadcasted_iota(i32, (n, N), 0) + (a - ROOT)
        t = (lax.broadcasted_iota(i32, (n, N), 1) & (BT - 1)) + within * BT
        return (p < branch_live) & (p <= t)

    def branch_tile(i):
        def make(slot):
            if i == 0:
                loads[1].wait()
                loads[4].wait()
            hs = [slice((4 * i + j) * D, (4 * i + j + 1) * D) for j in range(4)]
            tok = (lax.broadcasted_iota(i32, (4 * BT, 1), 0) & (BT - 1)) + within * BT
            do = jnp.where(tok < branch_live, grab(bg, hs), jnp.zeros((), bf16))
            col = (lax.broadcasted_iota(i32, (1, 4 * BT), 1) & (BT - 1)) + within * BT
            done = writer(hs, BT, ba, bdq, (1, 4) if i == 1 else ())
            return Tile(slot, grab(bq, hs), do, ROOT + BRANCH, col < branch_live, branch_mask, done)
        return make

    RT = 16
    def root_mask(a, n, N):
        t = (lax.broadcasted_iota(i32, (n, N), 1) & (RT - 1)) + leaf_index * RT
        return lax.broadcasted_iota(i32, (n, N), 0) + a <= t
    def root_tile(slot):
        loads[0].wait()
        loads[3].wait()
        hs = [slice(j * D, (j + 1) * D) for j in range(HG)]
        live = lax.broadcasted_iota(i32, (1, HG * RT), 1) >= 0
        done = writer(hs, RT, ra, rdq, (0, 3))
        return Tile(slot, grab(rq, hs), grab(rg, hs), ROOT, live, root_mask, done)

    makers = [leaf_tile(i) for i in range(4)] + [branch_tile(i) for i in range(2)] + [root_tile]
    tiles = {}
    for t in range(-2, len(makers)):
        jobs = []
        if t + 2 < len(makers):
            tiles[t + 2] = makers[t + 2]((t + 2) % 3)
        for at, job in ((t, 'spread'), (t + 1, 'weigh'), (t + 2, 'score')):
            if 0 <= at < len(makers):
                jobs.append((getattr(tiles[at], job), chunks(tiles[at].nk)))
        for i in range(7):
            for job, parts in jobs:
                if i < len(parts):
                    job(*parts[i])
        if 0 <= t + 1 < len(makers):
            tiles[t + 1].norm()
        if t >= 0:
            tiles[t].finish()
    ldk[...] = (ak[ROOT + BRANCH:, :] * SCALE).astype(bf16)
    ldv[...] = av[ROOT + BRANCH:, :].astype(bf16)
    stores[6].start()
    stores[7].start()

    for s, r in zip(root_rows + branch_rows, (r0o, r1o, r2o, r3o, b0o, b1o)):
        r[:, :D] = (ak[s, :] * SCALE).astype(r.dtype)
        r[:, D:] = av[s, :].astype(r.dtype)
    for c in stores:
        c.wait()


def attend(where, g, lengths, queries, grads, roots, branch, lk, lv, prev=None):
    W = HG * D
    def col(rows, w):
        return pl.BlockSpec((rows, w), lambda i: (0, g))
    def whole(shape):
        return pl.BlockSpec(shape, lambda i: (0, 0))
    in_specs = [pl.BlockSpec(memory_space=pltpu.SMEM)] * 2
    far = pl.BlockSpec(memory_space=pltpu.HBM)
    in_specs += [far] * 8
    in_specs += [whole((256, 2 * D))] * 4 + [col(256, 2 * D)] * 2
    args = [*lengths, *queries, *grads, lk, lv, *roots, *branch]
    alias = {}
    if prev is not None:
        for i, p in enumerate(prev):
            alias[len(args)] = i
            args.append(p)
            in_specs.append(far)
    S = jax.ShapeDtypeStruct
    outs = [S((n, 2 * W), bf16) for n in (16, 64, 128)] * 2 + [S((LEAF, 2 * D), bf16)] * 2
    out_specs = [far] * 8
    outs += [S((256, 2 * D), f32)] + [S((256, 2 * D), bf16)] * 3
    outs += [S((256, 2 * D), f32), S((256, 2 * D), bf16)]
    out_specs += [whole((256, 2 * D))] * 6
    near = [pltpu.VMEM((n, W), bf16) for n in (16, 64, 128)] * 2 + [pltpu.VMEM((LEAF, D), bf16)] * 2
    scratch = near + near + [pltpu.VMEM((KEYS, D), bf16)] * 2 + [pltpu.VMEM((D, KEYS), bf16)] * 2
    scratch += [pltpu.VMEM((3, KEYS, 256), f32)] * 2 + [pltpu.VMEM((KEYS, D), f32)] * 2
    scratch += [pltpu.SemaphoreType.DMA((8,))] * 2
    return pl.pallas_call(
        functools.partial(attend_kernel, where, g), grid=(1,), out_shape=outs, in_specs=in_specs, out_specs=out_specs,
        scratch_shapes=scratch, input_output_aliases=alias,
        compiler_params=pltpu.CompilerParams(vmem_limit_bytes=28 * 2**20),
        cost_estimate=pl.CostEstimate(flops=2 * 6 * 1664 * 1664 * 128, bytes_accessed=6 * 2**20, transcendentals=1664 * 1664),
        name="attend",
    )(*args)


def pack(rk, rv, raw):
    for g in range(2):
        for j, r in enumerate((rk, rv)):
            to = slice((2 * g + j) * D, (2 * g + j + 1) * D)
            for h in range(4):
                part = r[:, (2 * h + g) * D:(2 * h + g + 1) * D]
                for i in range(0, raw.shape[0], 4):
                    raw[i + h, :, to] = part


def pack_branch(bk, bv, mine):
    for g in range(2):
        for j, r in enumerate((bk, bv)):
            mine[:, (2 * g + j) * D:(2 * g + j + 1) * D] = r[:, g * D:(g + 1) * D]


def slot(axis, d, n):
    at = (lax.axis_index(axis) - d) & 3
    return pl.ds(pl.multiple_of(at * n, n), n)


def halves(own, o0, o1):
    o0[...] = own[:, :2 * D]
    o1[...] = own[:, 2 * D:]


def join_z(after, r0, r1, r2, r3, o):
    for d, r in enumerate((r0, r1, r2, r3)):
        o[slot("z", d, r.shape[0]), :] = r[...]


def total(own, parts, s=slice(None)):
    t = own[s, :]
    for p in parts:
        t = t + p[s, :].astype(f32)
    return t


def add_y(own0, a1, a2, a3, own1, c1, c2, c3, o):
    n = o.shape[1]
    for g, (own, *parts) in enumerate(((own0, a1, a2, a3), (own1, c1, c2, c3))):
        t = total(own, parts).astype(o.dtype)
        for i in range(o.shape[0]):
            o[i, :, 2 * g * D:2 * (g + 1) * D] = t[i * n:(i + 1) * n]


def add_pair(own0, a1, own1, c1, *outs):
    n = outs[0].shape[0]
    for g, (own, part) in enumerate(((own0, a1), (own1, c1))):
        for d, out in enumerate(outs):
            t = total(own, (part,), slot("z", d, n))
            out[:, 2 * g * D:2 * (g + 1) * D] = t.astype(out.dtype)


def add_z(own, a1, a2, a3, ok, ov):
    t = total(own, (a1, a2, a3))
    for g in range(2):
        ok[:, g * D:(g + 1) * D] = t[:, 2 * g * D:(2 * g + 1) * D].astype(ok.dtype)
        ov[:, g * D:(g + 1) * D] = t[:, (2 * g + 1) * D:(2 * g + 2) * D].astype(ov.dtype)


def add_last(parts, ok, ov):
    for h in range(4):
        t = parts[h].astype(f32)
        for i in range(4, parts.shape[0], 4):
            t = t + parts[i + h].astype(f32)
        for g in range(2):
            to = slice((2 * h + g) * D, (2 * h + g + 1) * D)
            ok[:, to] = t[:, 2 * g * D:(2 * g + 1) * D].astype(ok.dtype)
            ov[:, to] = t[:, (2 * g + 1) * D:(2 * g + 2) * D].astype(ov.dtype)


def small(body, outs, *args, grant=12, flops=10**6):
    def whole(shape):
        return pl.BlockSpec(shape, lambda i: (0,) * len(shape))
    return pl.pallas_call(
        body,
        grid=(1,),
        out_shape=[jax.ShapeDtypeStruct(s, t) for s, t in outs],
        in_specs=[whole(a.shape) for a in args],
        out_specs=[whole(s) for s, _ in outs],
        compiler_params=pltpu.CompilerParams(vmem_limit_bytes=grant * 2**20),
        cost_estimate=pl.CostEstimate(flops=flops, bytes_accessed=2**20, transcendentals=0),
    )(*args)


def shift(a, axis, d):
    return lax.ppermute(a, axis, [(i, (i + d) % 4) for i in range(4)])


def shifts(a, axis):
    return [shift(a, axis, d) for d in (1, 2, 3)]


def back(parts, axis):
    return [shift(p, axis, -d) for d, p in zip((1, 2, 3), parts)]


def pair(a):
    return lax.ppermute(a, "x", [(i, i ^ 1) for i in range(4)])


def local(
    root_query, branch_query, leaf_query, root_key, root_value, branch_key, branch_value,
    leaf_key, leaf_value, root_grad_out, branch_grad_out, leaf_grad_out,
    branch_lengths, leaf_lengths,
):
    where = lambda: tuple(lax.axis_index(a) for a in ("y", "x", "z"))
    lengths = (branch_lengths, leaf_lengths)
    queries = (root_query, branch_query, leaf_query)
    grads = (root_grad_out, branch_grad_out, leaf_grad_out)

    raw, = small(pack, [((64, 4, 4 * D), bf16)], root_key, root_value, grant=56)
    own = lax.all_to_all(raw, ("x", "z", "head"), 0, 0, tiled=True).reshape(256, 4 * D)
    r0, r1 = small(halves, [((256, 2 * D), bf16)] * 2, own)
    mine, = small(pack_branch, [((64, 4 * D), bf16)], branch_key, branch_value, grant=56, flops=4 * 10**10)
    mine, = small(join_z, [((256, 4 * D), bf16)], r1, mine, *shifts(mine, "z"))

    branch = (mine, pair(mine))
    roots0 = [r0, *shifts(r0, "y")]
    r1, *roots0 = lax.optimization_barrier((r1, *roots0))
    roots1 = [r1, *shifts(r1, "y")]

    first = attend(where, 0, lengths, queries, grads, roots0, branch, leaf_key, leaf_value)
    y0, roots1 = lax.optimization_barrier((first[9:12], roots1))
    y0 = back(y0, "y")
    b0 = pair(first[13])
    second = attend(
        where, 1, lengths, queries, grads, roots1, branch, leaf_key, leaf_value, first[:8]
    )
    y1, b1, *rest = lax.optimization_barrier((second[9:12], second[13], *y0, b0))
    y0, b0 = rest[:3], rest[3]
    y1, b1 = back(y1, "y"), pair(b1)
    own, *parts = small(
        add_pair, [((64, 4 * D), f32)] + [((64, 4 * D), bf16)] * 3,
        first[12], b0, second[12], b1,
    )
    z1, z2, z3 = back(parts, "z")
    sums, = small(add_y, [((64, 4, 4 * D), bf16)], first[8], *y0, second[8], *y1)
    sums, z1, z2, z3 = lax.optimization_barrier((sums, z1, z2, z3))
    bk, bv = small(add_z, [((64, 2 * D), bf16)] * 2, own, z1, z2, z3)
    last = lax.all_to_all(sums, ("x", "z", "head"), 0, 0, tiled=True)
    rk, rv = small(add_last, [((4, 8 * D), bf16)] * 2, last)
    ra, ba, la, rdq, bdq, ldq, ldk, ldv = second[:8]
    return ra, ba, la, rdq, bdq, ldq, rk, rv, bk, bv, ldk, ldv


def solution(mesh):
    fine = Mesh(mesh.devices.reshape(4, 4, 4, 4), ("y", "x", "z", "head"))
    leaf = ("y", "x", "z")
    both, rows = P(leaf, "head"), P((*leaf, "head"), None)
    return jax.shard_map(
        local,
        mesh=fine,
        in_specs=(both, both, both, rows, rows, both, both, both, both, both, both, both, P(), P(leaf)),
        out_specs=(both, both, both, both, both, both, rows, rows, both, both, both, both),
        check_vma=False,
    )
```

```python
import functools, math
import jax, jax.numpy as jnp
from jax import lax
from jax.experimental import pallas as pl
from jax.experimental.pallas import tpu as pltpu
from jax.sharding import Mesh, PartitionSpec as P

D = 128
HG = 8
GROUP = 8
ROOT, BRANCH, LEAF = 1024, 512, 128
KEYS = ROOT + BRANCH + LEAF
NEG = -1e30
bf16, f32, i32 = jnp.bfloat16, jnp.float32, jnp.int32
SCALE = 1.0 / math.sqrt(D)
C2 = SCALE * math.log2(math.e)
NT = (((1,), (1,)), ((), ()))
NN = (((1,), (0,)), ((), ()))
CH = 256


def dot(a, b, dims=NN):
    return lax.dot_general(a, b, dims, preferred_element_type=f32)


def chunks(n):
    return [(a, min(CH, n - a)) for a in range(0, n, CH)]


def attend_kernel(where, g, branch_lengths, leaf_lengths, *rest):
    far_in, (r0, r1, r2, r3, b0, b1) = rest[:8], rest[8:14]
    rest = rest[-40:]
    far_out, (r0o, r1o, r2o, r3o, b0o, b1o) = rest[:8], rest[8:14]
    near_in, near_out = rest[14:22], rest[22:30]
    kk, vv, kt, vt, ss, dd, ak, av, sem_in, sem_out = rest[30:]
    rq, bq, lq, rg, bg, lg, lk, lv = near_in
    ra, ba, la, rdq, bdq, ldq, ldk, ldv = near_out

    def columns(ref, width):
        return ref.at[:, pl.ds(g * width, width)]

    loads = [pltpu.make_async_copy(columns(f, n.shape[1]), n, sem_in.at[i])
             for i, (f, n) in enumerate(zip(far_in, near_in))]
    stores = [pltpu.make_async_copy(n, columns(f, n.shape[1]), sem_out.at[i])
              for i, (f, n) in enumerate(zip(far_out, near_out))]
    for i in (6, 7, 2, 5, 1, 4, 0, 3):
        loads[i].start()
    y, x, z = where()
    within = (x & 1) * 4 + z
    leaf_index = y * 16 + x * 4 + z
    branch_live, leaf_live = branch_lengths[leaf_index // GROUP], leaf_lengths[0]
    def rows_at(n, start):
        return pl.ds(pl.multiple_of(start, n), n)
    root_rows = [rows_at(256, ((y - i) & 3) * 256) for i in range(4)]
    branch_rows = [rows_at(256, ROOT + ((x ^ i) & 1) * 256) for i in range(2)]
    for s, r in zip(root_rows + branch_rows, (r0, r1, r2, r3, b0, b1)):
        kk[s, :] = r[:, :D]
        vv[s, :] = r[:, D:]
    loads[6].wait()
    loads[7].wait()
    kk[ROOT + BRANCH:, :] = lk[...]
    vv[ROOT + BRANCH:, :] = lv[...]
    for a, n in chunks(KEYS):
        kt[:, a:a + n] = kk[a:a + n, :].astype(f32).T.astype(bf16)
        vt[:, a:a + n] = vv[a:a + n, :].astype(f32).T.astype(bf16)
    ak[...] = jnp.zeros_like(ak)
    av[...] = jnp.zeros_like(av)

    class Tile:
        def __init__(self, slot, q, do, nk, live, mask, done):
            self.q, self.do, self.nk, self.live, self.mask, self.done = q, do, nk, live, mask, done
            self.N = q.shape[0]
            self.ss, self.dd = ss.at[slot], dd.at[slot]
            self.m = jnp.full((1, self.N), NEG, f32)
            self.l = jnp.zeros((1, self.N), f32)
            self.dl = jnp.zeros((1, self.N), f32)
            self.ot = jnp.zeros((D, self.N), f32)
            self.qt = jnp.zeros((D, self.N), f32)

        def score(self, a, n):
            s = dot(kk[a:a + n, :], self.q, NT) * C2
            ok = self.mask(a, n, self.N)
            if ok is not None:
                s = jnp.where(ok, s, NEG)
            self.ss[a:a + n, :self.N] = s
            self.m = jnp.maximum(self.m, jnp.max(s, axis=0, keepdims=True))
            self.dd[a:a + n, :self.N] = dot(vv[a:a + n, :], self.do, NT)

        def weigh(self, a, n):
            e = jnp.exp2(self.ss[a:a + n, :self.N] - self.m)
            self.ss[a:a + n, :self.N] = e
            self.l = self.l + jnp.sum(e, axis=0, keepdims=True)
            self.dl = self.dl + jnp.sum(e * self.dd[a:a + n, :self.N], axis=0, keepdims=True)

        def norm(self):
            self.inv = 1.0 / self.l
            self.delta = self.dl * self.inv

        def spread(self, a, n):
            w = self.ss[a:a + n, :self.N] * self.inv
            p = w.astype(bf16)
            ds = (w * (self.dd[a:a + n, :self.N] - self.delta)).astype(bf16)
            av[a:a + n, :] += dot(p, self.do)
            ak[a:a + n, :] += dot(ds, self.q)
            self.ot = self.ot + dot(vt[:, a:a + n], p)
            self.qt = self.qt + dot(kt[:, a:a + n], ds)

        def finish(self):
            o = jnp.where(self.live, self.ot, 0.0).T.astype(bf16)
            self.done(o, (self.qt * SCALE).T.astype(bf16))

    def grab(ref, heads):
        return jnp.concatenate([ref[:, h] for h in heads], axis=0)

    def leaf_mask(a, n, N):
        if a < ROOT:
            return None
        if a < ROOT + BRANCH:
            return lax.broadcasted_iota(i32, (n, N), 0) + (a - ROOT) < branch_live
        k = lax.broadcasted_iota(i32, (n, N), 0)
        t = lax.broadcasted_iota(i32, (n, N), 1) & (LEAF - 1)
        return (k < leaf_live) & (k <= t)

    def writer(heads, T, o_ref, dq_ref, sent):
        def done(o, dq):
            for j, h in enumerate(heads):
                o_ref[:, h] = o[j * T:(j + 1) * T]
                dq_ref[:, h] = dq[j * T:(j + 1) * T]
            for i in sent:
                stores[i].start()
        return done

    def leaf_tile(i):
        def make(slot):
            if i == 0:
                loads[2].wait()
                loads[5].wait()
            hs = [slice((2 * i + j) * D, (2 * i + j + 1) * D) for j in range(2)]
            tok = lax.broadcasted_iota(i32, (2 * LEAF, 1), 0) & (LEAF - 1)
            do = jnp.where(tok < leaf_live, grab(lg, hs), jnp.zeros((), bf16))
            col = lax.broadcasted_iota(i32, (1, 2 * LEAF), 1) & (LEAF - 1)
            done = writer(hs, LEAF, la, ldq, (2, 5) if i == 3 else ())
            return Tile(slot, grab(lq, hs), do, KEYS, col < leaf_live, leaf_mask, done)
        return make

    BT = 64
    def branch_mask(a, n, N):
        if a < ROOT:
            return None
        p = lax.broadcasted_iota(i32, (n, N), 0) + (a - ROOT)
        t = (lax.broadcasted_iota(i32, (n, N), 1) & (BT - 1)) + within * BT
        return (p < branch_live) & (p <= t)

    def branch_tile(i):
        def make(slot):
            if i == 0:
                loads[1].wait()
                loads[4].wait()
            hs = [slice((4 * i + j) * D, (4 * i + j + 1) * D) for j in range(4)]
            tok = (lax.broadcasted_iota(i32, (4 * BT, 1), 0) & (BT - 1)) + within * BT
            do = jnp.where(tok < branch_live, grab(bg, hs), jnp.zeros((), bf16))
            col = (lax.broadcasted_iota(i32, (1, 4 * BT), 1) & (BT - 1)) + within * BT
            done = writer(hs, BT, ba, bdq, (1, 4) if i == 1 else ())
            return Tile(slot, grab(bq, hs), do, ROOT + BRANCH, col < branch_live, branch_mask, done)
        return make

    RT = 16
    def root_mask(a, n, N):
        t = (lax.broadcasted_iota(i32, (n, N), 1) & (RT - 1)) + leaf_index * RT
        return lax.broadcasted_iota(i32, (n, N), 0) + a <= t
    def root_tile(slot):
        loads[0].wait()
        loads[3].wait()
        hs = [slice(j * D, (j + 1) * D) for j in range(HG)]
        live = lax.broadcasted_iota(i32, (1, HG * RT), 1) >= 0
        done = writer(hs, RT, ra, rdq, (0, 3))
        return Tile(slot, grab(rq, hs), grab(rg, hs), ROOT, live, root_mask, done)

    makers = [leaf_tile(i) for i in range(4)] + [branch_tile(i) for i in range(2)] + [root_tile]
    tiles = {}
    for t in range(-2, len(makers)):
        jobs = []
        if t + 2 < len(makers):
            tiles[t + 2] = makers[t + 2]((t + 2) % 3)
        for at, job in ((t, 'spread'), (t + 1, 'weigh'), (t + 2, 'score')):
            if 0 <= at < len(makers):
                jobs.append((getattr(tiles[at], job), chunks(tiles[at].nk)))
        for i in range(7):
            for job, parts in jobs:
                if i < len(parts):
                    job(*parts[i])
        if 0 <= t + 1 < len(makers):
            tiles[t + 1].norm()
        if t >= 0:
            tiles[t].finish()
    ldk[...] = (ak[ROOT + BRANCH:, :] * SCALE).astype(bf16)
    ldv[...] = av[ROOT + BRANCH:, :].astype(bf16)
    stores[6].start()
    stores[7].start()

    for s, r in zip(root_rows + branch_rows, (r0o, r1o, r2o, r3o, b0o, b1o)):
        r[:, :D] = (ak[s, :] * SCALE).astype(r.dtype)
        r[:, D:] = av[s, :].astype(r.dtype)
    for c in stores:
        c.wait()


def attend(where, g, lengths, queries, grads, roots, branch, lk, lv, prev=None):
    W = HG * D
    def col(rows, w):
        return pl.BlockSpec((rows, w), lambda i: (0, g))
    def whole(shape):
        return pl.BlockSpec(shape, lambda i: (0, 0))
    in_specs = [pl.BlockSpec(memory_space=pltpu.SMEM)] * 2
    far = pl.BlockSpec(memory_space=pltpu.HBM)
    in_specs += [far] * 8
    in_specs += [whole((256, 2 * D))] * 4 + [col(256, 2 * D)] * 2
    args = [*lengths, *queries, *grads, lk, lv, *roots, *branch]
    alias = {}
    if prev is not None:
        for i, p in enumerate(prev):
            alias[len(args)] = i
            args.append(p)
            in_specs.append(far)
    S = jax.ShapeDtypeStruct
    outs = [S((n, 2 * W), bf16) for n in (16, 64, 128)] * 2 + [S((LEAF, 2 * D), bf16)] * 2
    out_specs = [far] * 8
    outs += [S((256, 2 * D), f32)] + [S((256, 2 * D), bf16)] * 3
    outs += [S((256, 2 * D), f32), S((256, 2 * D), bf16)]
    out_specs += [whole((256, 2 * D))] * 6
    near = [pltpu.VMEM((n, W), bf16) for n in (16, 64, 128)] * 2 + [pltpu.VMEM((LEAF, D), bf16)] * 2
    scratch = near + near + [pltpu.VMEM((KEYS, D), bf16)] * 2 + [pltpu.VMEM((D, KEYS), bf16)] * 2
    scratch += [pltpu.VMEM((3, KEYS, 256), f32)] * 2 + [pltpu.VMEM((KEYS, D), f32)] * 2
    scratch += [pltpu.SemaphoreType.DMA((8,))] * 2
    return pl.pallas_call(
        functools.partial(attend_kernel, where, g), grid=(1,), out_shape=outs, in_specs=in_specs, out_specs=out_specs,
        scratch_shapes=scratch, input_output_aliases=alias,
        compiler_params=pltpu.CompilerParams(vmem_limit_bytes=28 * 2**20),
        cost_estimate=pl.CostEstimate(flops=2 * 6 * 1664 * 1664 * 128, bytes_accessed=6 * 2**20, transcendentals=1664 * 1664),
        name="attend",
    )(*args)


def pack(rk, rv, raw):
    for g in range(2):
        for j, r in enumerate((rk, rv)):
            to = slice((2 * g + j) * D, (2 * g + j + 1) * D)
            for h in range(4):
                part = r[:, (2 * h + g) * D:(2 * h + g + 1) * D]
                for i in range(0, raw.shape[0], 4):
                    raw[i + h, :, to] = part


def pack_branch(bk, bv, mine):
    for g in range(2):
        for j, r in enumerate((bk, bv)):
            mine[:, (2 * g + j) * D:(2 * g + j + 1) * D] = r[:, g * D:(g + 1) * D]


def slot(axis, d, n):
    at = (lax.axis_index(axis) - d) & 3
    return pl.ds(pl.multiple_of(at * n, n), n)


def halves(own, o0, o1):
    o0[...] = own[:, :2 * D]
    o1[...] = own[:, 2 * D:]


def join_z(after, r0, r1, r2, r3, o):
    for d, r in enumerate((r0, r1, r2, r3)):
        o[slot("z", d, r.shape[0]), :] = r[...]


def total(own, parts, s=slice(None)):
    t = own[s, :]
    for p in parts:
        t = t + p[s, :].astype(f32)
    return t


def add_first(own0, a1, a2, a3, own1, c1, c2, c3, e0, f0, e1, f1, o, *outs):
    n = o.shape[1]
    for g, (own, *parts) in enumerate(((own0, a1, a2, a3), (own1, c1, c2, c3))):
        t = total(own, parts).astype(o.dtype)
        for i in range(o.shape[0]):
            o[i, :, 2 * g * D:2 * (g + 1) * D] = t[i * n:(i + 1) * n]
    n = outs[0].shape[0]
    for g, (own, part) in enumerate(((e0, f0), (e1, f1))):
        for d, out in enumerate(outs):
            t = total(own, (part,), slot("z", d, n))
            out[:, 2 * g * D:2 * (g + 1) * D] = t.astype(out.dtype)


def add_z(own, a1, a2, a3, ok, ov):
    t = total(own, (a1, a2, a3))
    for g in range(2):
        ok[:, g * D:(g + 1) * D] = t[:, 2 * g * D:(2 * g + 1) * D].astype(ok.dtype)
        ov[:, g * D:(g + 1) * D] = t[:, (2 * g + 1) * D:(2 * g + 2) * D].astype(ov.dtype)


def add_last(parts, ok, ov):
    for h in range(4):
        t = parts[h].astype(f32)
        for i in range(4, parts.shape[0], 4):
            t = t + parts[i + h].astype(f32)
        for g in range(2):
            to = slice((2 * h + g) * D, (2 * h + g + 1) * D)
            ok[:, to] = t[:, 2 * g * D:(2 * g + 1) * D].astype(ok.dtype)
            ov[:, to] = t[:, (2 * g + 1) * D:(2 * g + 2) * D].astype(ov.dtype)


def small(body, outs, *args, grant=12, flops=10**6):
    def whole(shape):
        return pl.BlockSpec(shape, lambda i: (0,) * len(shape))
    return pl.pallas_call(
        body,
        grid=(1,),
        out_shape=[jax.ShapeDtypeStruct(s, t) for s, t in outs],
        in_specs=[whole(a.shape) for a in args],
        out_specs=[whole(s) for s, _ in outs],
        compiler_params=pltpu.CompilerParams(vmem_limit_bytes=grant * 2**20),
        cost_estimate=pl.CostEstimate(flops=flops, bytes_accessed=2**20, transcendentals=0),
    )(*args)


def shift(a, axis, d):
    return lax.ppermute(a, axis, [(i, (i + d) % 4) for i in range(4)])


def shifts(a, axis):
    return [shift(a, axis, d) for d in (1, 2, 3)]


def back(parts, axis):
    return [shift(p, axis, -d) for d, p in zip((1, 2, 3), parts)]


def pair(a):
    return lax.ppermute(a, "x", [(i, i ^ 1) for i in range(4)])


def local(
    root_query, branch_query, leaf_query, root_key, root_value, branch_key, branch_value,
    leaf_key, leaf_value, root_grad_out, branch_grad_out, leaf_grad_out,
    branch_lengths, leaf_lengths,
):
    where = lambda: tuple(lax.axis_index(a) for a in ("y", "x", "z"))
    lengths = (branch_lengths, leaf_lengths)
    queries = (root_query, branch_query, leaf_query)
    grads = (root_grad_out, branch_grad_out, leaf_grad_out)

    raw, = small(pack, [((64, 4, 4 * D), bf16)], root_key, root_value, grant=56)
    own = lax.all_to_all(raw, ("x", "z", "head"), 0, 0, tiled=True).reshape(256, 4 * D)
    r0, r1 = small(halves, [((256, 2 * D), bf16)] * 2, own)
    mine, = small(pack_branch, [((64, 4 * D), bf16)], branch_key, branch_value, grant=56, flops=4 * 10**10)
    mine, = small(join_z, [((256, 4 * D), bf16)], r1, mine, *shifts(mine, "z"))

    branch = (mine, pair(mine))
    roots0 = [r0, *shifts(r0, "y")]
    r1, *roots0 = lax.optimization_barrier((r1, *roots0))
    roots1 = [r1, *shifts(r1, "y")]

    first = attend(where, 0, lengths, queries, grads, roots0, branch, leaf_key, leaf_value)
    y0, roots1 = lax.optimization_barrier((first[9:12], roots1))
    y0 = back(y0, "y")
    b0 = pair(first[13])
    second = attend(
        where, 1, lengths, queries, grads, roots1, branch, leaf_key, leaf_value, first[:8]
    )
    y1, b1, *rest = lax.optimization_barrier((second[9:12], second[13], *y0, b0))
    y0, b0 = rest[:3], rest[3]
    y1, b1 = back(y1, "y"), pair(b1)
    sums, own, *parts = small(
        add_first,
        [((64, 4, 4 * D), bf16), ((64, 4 * D), f32)] + [((64, 4 * D), bf16)] * 3,
        first[8], *y0, second[8], *y1, first[12], b0, second[12], b1,
    )
    bk, bv = small(add_z, [((64, 2 * D), bf16)] * 2, own, *back(parts, "z"))
    last = lax.all_to_all(sums, ("x", "z", "head"), 0, 0, tiled=True)
    rk, rv = small(add_last, [((4, 8 * D), bf16)] * 2, last)
    ra, ba, la, rdq, bdq, ldq, ldk, ldv = second[:8]
    return ra, ba, la, rdq, bdq, ldq, rk, rv, bk, bv, ldk, ldv


def solution(mesh):
    fine = Mesh(mesh.devices.reshape(4, 4, 4, 4), ("y", "x", "z", "head"))
    leaf = ("y", "x", "z")
    both, rows = P(leaf, "head"), P((*leaf, "head"), None)
    return jax.shard_map(
        local,
        mesh=fine,
        in_specs=(both, both, both, rows, rows, both, both, both, both, both, both, both, P(), P(leaf)),
        out_specs=(both, both, both, both, both, both, rows, rows, both, both, both, both),
        check_vma=False,
    )
```
